32 devices in a mesh: row: 4 (over y, x), col: 8 (over z, core).
Axes of the slice: x: 2, y: 2, z: 4, core: 2. Of those that a mesh axis runs over, the one named last changes fastest.
Arguments:
- amplitudes: bfloat16 [6144, 4096], P('row', 'col'), may hold values from -6 to 6
- integrals: bfloat16 [4096, 4096], P('row', 'col'), may hold values from -0.125 to 0.125
- screen_mask: int32 [48, 32], P('row', 'col'), may hold values from 0 to 1, as said below
- tile_order: int32 [32], replicated, may hold values from 0 to 31, each once
Outputs:
- ladder: float32 [6144, 4096], P('row', 'col')
The draws below stay inside these ranges and needn't reach their ends.
Inputs may be any that keep to these rules, and one draw needn't show every extreme that they name: `screen_mask`: in every aligned block of 12 tile rows by 4 tile columns exactly 24 tiles survive; rows of tiles hold different numbers of them. `tile_order`: each number of 0 to 31 appears once.
All inputs are finite; a program needn't handle non-finite values.
Results may differ from the reference program's by a relative error of at most 0.0003.
Values may be sent and summed in bfloat16 or wider, within the bound.
No kernel may reach another device: no remote copies, remote signals or barrier semaphores. Data moves between devices by JAX's collectives and lax.ppermute only.
A program may use at most 256 MiB of HBM per device.

```python
import jax
import jax.numpy as jnp

TILE_PAIRS = 128
TILES_PER_ROW = 12
KTC = 4
CAP = 24
OCCUPIED_TILES = 48
CONTRACT_TILES = 32
OCCUPIED_PAIRS = 6144
NPAIRS = 4096
VIRTUAL_PAIRS = 4096


def draw_screen_mask(key, part):
    first_key, second_key = jax.random.split(jax.random.fold_in(key, 17))
    row_partitions = OCCUPIED_TILES // TILES_PER_ROW
    col_groups = CONTRACT_TILES // KTC
    block_size = TILES_PER_ROW * KTC
    levels = jax.random.randint(first_key, (row_partitions, TILES_PER_ROW, 1, 1), 0, 4)
    rolled = jax.random.randint(second_key, (row_partitions, TILES_PER_ROW, col_groups, KTC), 0, 4)
    scores = levels * 4 + rolled
    blocks = jnp.transpose(scores, (0, 2, 1, 3)).reshape(row_partitions, col_groups, block_size)
    position = jnp.arange(block_size, dtype=jnp.int32)
    distinct = (15 - blocks) * block_size + position
    ranks = jnp.argsort(jnp.argsort(distinct, axis=-1), axis=-1)
    keep_flags = (ranks < CAP).astype(jnp.int32).reshape(row_partitions, col_groups, TILES_PER_ROW, KTC)
    return jnp.transpose(keep_flags, (0, 2, 1, 3)).reshape(OCCUPIED_TILES, CONTRACT_TILES)


def level_of(key, extent, cuts, smallest, high):
    factor_of = 1.0
    for dim, blocks in cuts:
        draws = jax.random.uniform(jax.random.fold_in(jax.random.fold_in(key, 6), dim), (blocks,), jnp.float32, smallest / len(cuts), high / len(cuts))
        factor_of = factor_of * jnp.repeat(jnp.exp(draws), extent[dim] // blocks).reshape((-1,) + (1,) * (len(extent) - 1 - dim))
    return factor_of


def gaussian(rng, shape, deviation, limit, cuts=(), kind=jnp.bfloat16):
    drawn = deviation * jax.random.normal(rng, shape, jnp.float32)
    if cuts:
        drawn = drawn * level_of(rng, shape, cuts, -0.22, 0.18)
    return jnp.clip(drawn, -limit, limit).astype(kind)


def setup_inputs(seed: int = 0) -> dict:
    keys = jax.random.split(jax.random.key(seed), 5)
    return {
        "amplitudes": gaussian(keys[0], (OCCUPIED_PAIRS, VIRTUAL_PAIRS), 1.0, 6.0, ((0, 4), (1, 8))),
        "integrals": gaussian(keys[1], (VIRTUAL_PAIRS, NPAIRS), (VIRTUAL_PAIRS // 2) ** -0.5, 0.125, ((0, 4), (1, 8))),
        "screen_mask": draw_screen_mask(jax.random.fold_in(keys[4], 71), 0),
        "tile_order": jax.random.permutation(keys[3], CONTRACT_TILES).astype(jnp.int32),
    }


def reference(amplitudes, integrals, screen_mask, tile_order):
    weight_values = screen_mask.astype(jnp.bfloat16)[:, None, :, None]
    screened_tiles = (amplitudes.reshape(OCCUPIED_TILES, TILE_PAIRS, CONTRACT_TILES, TILE_PAIRS) * weight_values).reshape(OCCUPIED_PAIRS, VIRTUAL_PAIRS)
    ordered = jnp.take(integrals.reshape(CONTRACT_TILES, TILE_PAIRS, NPAIRS), tile_order.astype(jnp.int32), axis=0).reshape(VIRTUAL_PAIRS, NPAIRS)
    return jnp.dot(screened_tiles, ordered, preferred_element_type=jnp.float32)
```

```python
import functools

import jax
import jax.numpy as jnp
from jax import lax
from jax.experimental import pallas as pl
from jax.experimental.pallas import tpu as pltpu
from jax.sharding import PartitionSpec as P

TILE = 128
CAP = 24
META = 16
ROWS = 512
LANES = 128
SWAP = CAP * TILE + META
BLOCK = SWAP + META
SMEM = pl.BlockSpec(memory_space=pltpu.SMEM)
VMEM = pl.BlockSpec(memory_space=pltpu.VMEM)
ANY = pl.BlockSpec(memory_space=pl.ANY)


ORDER = {
    ("line", 2, 0): [("swap", 0, 0)],
    ("line", 2, 1): [("swap", 1, 0), ("side", 1, 0), ("side", 2, 0)],
    ("swap", 2, 1): [("side", 3, 0)],
    ("swap", 1, 1): [("line", 2, 0)],
}


def nbytes(shape, dtype):
    size = jnp.dtype(dtype).itemsize
    for extent in shape:
        size *= extent
    return size


def with_vmem(arrays):
    need = sum(nbytes(shape, dtype) for shape, dtype in arrays)
    return pltpu.CompilerParams(vmem_limit_bytes=need + 6 * 1024 * 1024)


def in_hbm(x):
    return pltpu.with_memory_space_constraint(x, pltpu.HBM)


def in_vmem(x):
    return pltpu.with_memory_space_constraint(x, pltpu.VMEM)


def dot(left, right):
    return jnp.dot(left, right, preferred_element_type=jnp.float32)


def pack_kernel(mask_hbm, amplitudes_ref, packed, mask_ref, amplitudes, mask_sem, in_sems):
    col_tiles, row_tiles = mask_ref.shape
    mask_copy = pltpu.make_async_copy(mask_hbm, mask_ref, mask_sem)
    mask_copy.start()
    copies = []
    for i in range(row_tiles):
        at = pl.ds(i * TILE, TILE)
        copies.append(
            pltpu.make_async_copy(amplitudes_ref.at[at], amplitudes.at[at], in_sems.at[i])
        )
        copies[i].start()
    lane = lax.broadcasted_iota(jnp.int32, (META, LANES), 1)
    places = jnp.full((META, LANES), CAP, jnp.int32)
    slot = jnp.int32(0)
    mask_copy.wait()
    for i in range(row_tiles):
        copies[i].wait()
        for k in range(col_tiles):
            keep = mask_ref[k, i] != 0

            @pl.when(keep)
            def _(i=i, k=k, slot=slot):
                to = pl.ds(pl.multiple_of(slot * TILE, TILE), TILE)
                packed[to] = amplitudes[pl.ds(i * TILE, TILE), pl.ds(k * TILE, TILE)]

            places = jnp.where(lane == i * col_tiles + k, jnp.where(keep, slot, CAP), places)
            slot = slot + keep.astype(jnp.int32)
    packed[pl.ds(CAP * TILE, META)] = places.astype(jnp.float32).astype(packed.dtype)


def pack(mask, amplitudes):
    shape = (BLOCK, TILE)
    dtype = amplitudes.dtype
    return pl.pallas_call(
        pack_kernel,
        out_shape=pltpu.VMEM(shape, dtype),
        in_specs=[ANY, ANY],
        out_specs=VMEM,
        scratch_shapes=[
            pltpu.SMEM(mask.shape[::-1], mask.dtype),
            pltpu.VMEM(amplitudes.shape, dtype),
            pltpu.SemaphoreType.DMA,
            pltpu.SemaphoreType.DMA((mask.shape[0],)),
        ],
        compiler_params=with_vmem([(amplitudes.shape, dtype)]),
        cost_estimate=pl.CostEstimate(
            flops=0, bytes_accessed=3 * nbytes(shape, dtype), transcendentals=0
        ),
        name="pack",
    )(in_hbm(mask.T), in_hbm(amplitudes))


def unpacked(places_ref, table, rows, packed, col_tiles):
    lines = []
    for i in range(ROWS // TILE):
        line = []
        for k in range(col_tiles):
            place = places_ref[table, 0, (rows * (ROWS // TILE) + i) * col_tiles + k]
            at = pl.multiple_of(jnp.minimum(place, CAP - 1) * TILE, TILE)
            tile = packed[pl.ds(at, TILE)]
            line.append(jnp.where(place < CAP, tile, jnp.zeros_like(tile)))
        lines.append(jnp.concatenate(line, axis=1))
    return jnp.concatenate(lines, axis=0)


def places_of(packed):
    return packed[pl.ds(CAP * TILE, META)].astype(jnp.float32).astype(jnp.int32)[:8]


def near_kernel(chips, row_devices, steps, b_count, order_ref, *refs):
    refs = list(refs)
    pieces = [(refs.pop(0), refs.pop(0)) for _ in steps]
    b_refs = [refs.pop(0) for _ in range(b_count)]
    total, far_rows, b_all, ordered, places_vmem, places, places_sem = refs

    row = lax.axis_index("row")
    col = lax.axis_index("col")
    chip, core = col // 2, col % 2
    b_tiles = b_all.shape[0] // row_devices // TILE
    col_tiles = ordered.shape[0] // TILE // 2

    for e, piece in enumerate(pieces):
        for side, ref in enumerate(piece):
            places_vmem[2 * e + side] = places_of(ref)
    places_copy = pltpu.make_async_copy(places_vmem, places, places_sem)
    places_copy.start()
    total[...] = jnp.zeros_like(total)
    start = 0
    for ref in b_refs:
        size = ref.shape[0]
        b_all[pl.ds(start, size)] = ref[...]
        start += size

    def order_rows(from_chip, first_core, into):
        for side in range(2):
            for k in range(col_tiles):
                place = first_core if side == 0 else 1 - first_core
                tile = order_ref[(from_chip * 2 + place) * col_tiles + k]
                at = ((tile // b_tiles) ^ row) * b_tiles + tile % b_tiles
                into[pl.ds((side * col_tiles + k) * TILE, TILE)] = b_all[
                    pl.ds(pl.multiple_of(at * TILE, TILE), TILE)
                ]

    order_rows(jnp.where(chip == 0, chips - 1, 0), 0, far_rows)
    places_copy.wait()

    for e, step in enumerate(steps):
        source = chip + (2 * core - 1) * step

        @pl.when((source >= 0) & (source < chips))
        def _(e=e, step=step, source=source):
            order_rows(source, core if step >= 0 else 1 - core, ordered)

            @pl.loop(0, total.shape[0] // ROWS)
            def _(m):
                at = pl.ds(pl.multiple_of(m * ROWS, ROWS), ROWS)
                left = [
                    unpacked(places, 2 * e + side, m, pieces[e][side], col_tiles)
                    for side in range(2)
                ]
                total[at] += dot(jnp.concatenate(left, axis=1), ordered[...])


def near(chips, row_devices, steps, order, pieces, b_parts, shape, col_tiles):
    local_rows, result_cols = shape
    dtype = b_parts[0].dtype
    depth = 2 * col_tiles * TILE
    flat = [chunk for piece in pieces for chunk in piece] + b_parts
    blocks = 2 * len(steps)
    b_rows = sum(part.shape[0] for part in b_parts)
    scratch = [
        ((b_rows, result_cols), dtype),
        ((depth, result_cols), dtype),
        ((blocks, 8, LANES), jnp.int32),
    ]
    outs = [(shape, jnp.float32), ((depth, result_cols), dtype)]
    return pl.pallas_call(
        functools.partial(near_kernel, chips, row_devices, steps, len(b_parts)),
        out_shape=[pltpu.VMEM(*entry) for entry in outs],
        in_specs=[SMEM] + [VMEM] * len(flat),
        out_specs=[VMEM] * 2,
        scratch_shapes=[pltpu.VMEM(*entry) for entry in scratch] + [
            pltpu.SMEM((blocks, 8, LANES), jnp.int32),
            pltpu.SemaphoreType.DMA,
        ],
        compiler_params=with_vmem(scratch),
        cost_estimate=pl.CostEstimate(flops=0, bytes_accessed=0, transcendentals=0),
        name="near",
    )(in_hbm(order), *[in_vmem(x) for x in flat])


def far_kernel(chips, block, last, mine, other, far_rows, total_in, total_out, *refs):
    refs = list(refs)
    total = refs.pop(0) if last else total_out
    places_vmem, places, places_sem = refs[:3]
    col = lax.axis_index("col")
    chip, core = col // 2, col % 2
    depth = far_rows.shape[0] // 2
    outs = [None] * (total.shape[0] // ROWS)
    if last:
        for m in range(len(outs)):
            at = pl.ds(m * ROWS, ROWS)
            outs[m] = pltpu.make_async_copy(total.at[at], total_out.at[at], refs[3].at[m])

    for ref, stream in ((mine, core), (other, 1 - core)):

        @pl.when(chip == (chips - 1) * (1 - stream))
        def _(ref=ref, stream=stream):
            places_vmem[...] = places_of(ref)
            copy = pltpu.make_async_copy(places_vmem, places.at[0], places_sem)
            copy.start()
            start = pl.multiple_of((stream ^ block) * depth, depth)
            right = far_rows[pl.ds(start, depth)]
            copy.wait()
            for m, out in enumerate(outs):
                at = pl.ds(m * ROWS, ROWS)
                total[at] = total_in[at] + dot(unpacked(places, 0, m, ref, depth // TILE), right)
                if last:
                    out.start()

    if last:

        @pl.when((chip != 0) & (chip != chips - 1))
        def _():
            for m, out in enumerate(outs):
                at = pl.ds(m * ROWS, ROWS)
                total[at] = total_in[at]
                out.start()

        for out in outs:
            out.wait()


def far(chips, block, mine, other, far_rows, total, last):
    shape = total.shape
    local_rows, result_cols = shape
    scratch = [((8, LANES), jnp.int32)]
    if last:
        scratch.insert(0, (shape, jnp.float32))
    sems = [pltpu.SemaphoreType.DMA((local_rows // ROWS,))] if last else []
    return pl.pallas_call(
        functools.partial(far_kernel, chips, block, last),
        out_shape=(pltpu.HBM if last else pltpu.VMEM)(shape, jnp.float32),
        in_specs=[VMEM] * 4,
        out_specs=ANY if last else VMEM,
        input_output_aliases={} if last else {3: 0},
        scratch_shapes=[pltpu.VMEM(*entry) for entry in scratch] + [
            pltpu.SMEM((1, 8, LANES), jnp.int32),
            pltpu.SemaphoreType.DMA,
        ] + sems,
        compiler_params=with_vmem(scratch),
        cost_estimate=pl.CostEstimate(
            flops=local_rows * result_cols * far_rows.shape[0], bytes_accessed=8 * 1024 * 1024,
            transcendentals=0,
        ),
        name="far",
    )(*[in_vmem(x) for x in (mine, other, far_rows, total)])


def after(chunk, others):
    return lax.optimization_barrier((chunk, *others))[0] if others else chunk


class Transfers:
    def __init__(self, row_devices, chips, own, integrals):
        self.row_devices = row_devices
        self.chips = chips
        self.integrals = integrals
        self.made = {("own", 0, 0): own, ("side", 0, 0): integrals}

    def get(self, name):
        if name not in self.made:
            self.made[name] = getattr(self, name[0])(name, *name[1:])
        return self.made[name]

    def held(self, name):
        return name[1] < (self.row_devices if name[0] == "side" else self.chips)

    def send(self, chunk, axis, perm, name):
        others = [self.get(other) for other in ORDER.get(name, ()) if self.held(other)]
        return lax.ppermute(after(chunk, others), axis, perm)

    def line(self, name, step, i):
        cross = i if step == 1 else 0
        below, above = range(step, self.chips), range(self.chips - step)
        perm = [(2 * (z - 1) + cross, 2 * z) for z in below]
        perm += [(2 * (z + 1) + 1 - cross, 2 * z + 1) for z in above]
        chunk = self.get(("own", 0, 0) if step == 1 else ("line", step - 1, i))
        return self.send(chunk, "col", perm, name)

    def swap(self, name, step, i):
        perm = [(2 * z, 2 * z + 1) for z in range(step, self.chips)]
        perm += [(2 * z + 1, 2 * z) for z in range(self.chips - step)]
        chunk = self.get(("line", step, i) if step else ("own", 0, 0))[:SWAP]
        return self.send(chunk, "col", perm, name)

    def half(self, d, h):
        if d & (d - 1):
            return self.get(("side", d, h))
        rows = self.integrals.shape[0] // 2
        return self.get(("side", d, 0))[h * rows : (h + 1) * rows]

    def side(self, name, d, h):
        if d & (d - 1):
            bit = d & -d if h else 1 << (d.bit_length() - 1)
            chunk = self.half(d ^ bit, h)
        else:
            bit, chunk = d, self.integrals
        perm = [(r, r ^ bit) for r in range(self.row_devices)]
        return self.send(chunk, "row", perm, name)


def local(row_devices, col_devices, amplitudes, integrals, screen_mask, tile_order):
    chips = col_devices // 2
    own = pack(screen_mask, amplitudes)
    moves = Transfers(row_devices, chips, own, integrals)
    sides = [("side", d, h) for d in range(row_devices) for h in range(2 if d & (d - 1) else 1)]
    steps = [0]
    pieces = [(own, moves.get(("swap", 0, 0)))]
    for step in range(1, chips - 1):
        for kind in ("line", "swap"):
            steps.append(step if kind == "line" else -step)
            pieces.append([moves.get((kind, step, i)) for i in range(2)])
    total, far_rows = near(
        chips, row_devices, steps, tile_order, pieces, [moves.get(side) for side in sides],
        (amplitudes.shape[0], integrals.shape[1]), screen_mask.shape[1],
    )
    last = []
    for i in range(2):
        name = ("line", chips - 1, i)
        moves.made[name], total = lax.optimization_barrier((moves.get(name), total))
        last.append((moves.made[name], moves.get(("swap", chips - 1, i))))
    for i, (block, other) in enumerate(last):
        total = far(chips, i, block, other, far_rows, total, i == len(last) - 1)
    return total


def solution(mesh):
    placed = (P("row", "col"), P("row", "col"), P("row", "col"), P())
    return jax.shard_map(
        functools.partial(local, mesh.shape["row"], mesh.shape["col"]),
        mesh=mesh, in_specs=placed, out_specs=P("row", "col"), check_vma=False,
    )
```

```python
import functools

import jax
import jax.numpy as jnp
from jax import lax
from jax.experimental import pallas as pl
from jax.experimental.pallas import tpu as pltpu
from jax.sharding import PartitionSpec as P

TILE = 128
CAP = 24
META = 16
ROWS = 512
LAST_ROWS = 256
LANES = 128
SWAP = CAP * TILE + META
BLOCK = SWAP + META
SMEM = pl.BlockSpec(memory_space=pltpu.SMEM)
VMEM = pl.BlockSpec(memory_space=pltpu.VMEM)
ANY = pl.BlockSpec(memory_space=pl.ANY)


ORDER = {
    ("line", 2, 0): [("swap", 0, 0)],
    ("line", 2, 1): [("swap", 1, 0), ("side", 1, 0), ("side", 2, 0)],
    ("swap", 2, 1): [("side", 3, 0)],
    ("swap", 1, 1): [("line", 2, 0)],
}


def nbytes(shape, dtype):
    size = jnp.dtype(dtype).itemsize
    for extent in shape:
        size *= extent
    return size


def with_vmem(arrays):
    need = sum(nbytes(shape, dtype) for shape, dtype in arrays)
    return pltpu.CompilerParams(vmem_limit_bytes=need + 6 * 1024 * 1024)


def in_hbm(x):
    return pltpu.with_memory_space_constraint(x, pltpu.HBM)


def in_vmem(x):
    return pltpu.with_memory_space_constraint(x, pltpu.VMEM)


def dot(left, right):
    return jnp.dot(left, right, preferred_element_type=jnp.float32)


def pack_kernel(mask_hbm, amplitudes_ref, packed, mask_ref, amplitudes, mask_sem, in_sems):
    col_tiles, row_tiles = mask_ref.shape
    mask_copy = pltpu.make_async_copy(mask_hbm, mask_ref, mask_sem)
    mask_copy.start()
    copies = []
    for i in range(row_tiles):
        at = pl.ds(i * TILE, TILE)
        copies.append(
            pltpu.make_async_copy(amplitudes_ref.at[at], amplitudes.at[at], in_sems.at[i])
        )
        copies[i].start()
    lane = lax.broadcasted_iota(jnp.int32, (META, LANES), 1)
    places = jnp.full((META, LANES), CAP, jnp.int32)
    slot = jnp.int32(0)
    mask_copy.wait()
    for i in range(row_tiles):
        copies[i].wait()
        for k in range(col_tiles):
            keep = mask_ref[k, i] != 0

            def store(i=i, k=k, slot=slot):
                to = pl.ds(pl.multiple_of(slot * TILE, TILE), TILE)
                packed[to] = amplitudes[pl.ds(i * TILE, TILE), pl.ds(k * TILE, TILE)]

            if i * col_tiles + k < CAP:
                store()
            else:
                pl.when(keep)(store)

            places = jnp.where(lane == i * col_tiles + k, jnp.where(keep, slot, CAP), places)
            slot = slot + keep.astype(jnp.int32)
    packed[pl.ds(CAP * TILE, META)] = places.astype(jnp.float32).astype(packed.dtype)


def pack(mask, amplitudes):
    shape = (BLOCK, TILE)
    dtype = amplitudes.dtype
    return pl.pallas_call(
        pack_kernel,
        out_shape=pltpu.VMEM(shape, dtype),
        in_specs=[ANY, ANY],
        out_specs=VMEM,
        scratch_shapes=[
            pltpu.SMEM(mask.shape[::-1], mask.dtype),
            pltpu.VMEM(amplitudes.shape, dtype),
            pltpu.SemaphoreType.DMA,
            pltpu.SemaphoreType.DMA((mask.shape[0],)),
        ],
        compiler_params=with_vmem([(amplitudes.shape, dtype)]),
        cost_estimate=pl.CostEstimate(
            flops=0, bytes_accessed=3 * nbytes(shape, dtype), transcendentals=0
        ),
        name="pack",
    )(in_hbm(mask.T), in_hbm(amplitudes))


def unpacked(places_ref, table, rows, packed, col_tiles, height=ROWS):
    lines = []
    for i in range(height // TILE):
        line = []
        for k in range(col_tiles):
            place = places_ref[table, 0, (rows * (height // TILE) + i) * col_tiles + k]
            at = pl.multiple_of(jnp.minimum(place, CAP - 1) * TILE, TILE)
            tile = packed[pl.ds(at, TILE)]
            line.append(jnp.where(place < CAP, tile, jnp.zeros_like(tile)))
        lines.append(jnp.concatenate(line, axis=1))
    return jnp.concatenate(lines, axis=0)


def places_of(packed):
    return packed[pl.ds(CAP * TILE, META)].astype(jnp.float32).astype(jnp.int32)[:8]


def near_kernel(chips, row_devices, steps, b_count, order_ref, *refs):
    refs = list(refs)
    pieces = [(refs.pop(0), refs.pop(0)) for _ in steps]
    b_refs = [refs.pop(0) for _ in range(b_count)]
    total, far_rows, b_all, ordered, places_vmem, places, places_sem = refs

    row = lax.axis_index("row")
    col = lax.axis_index("col")
    chip, core = col // 2, col % 2
    b_tiles = b_all.shape[0] // row_devices // TILE
    col_tiles = ordered.shape[0] // TILE // 2

    for e, piece in enumerate(pieces):
        for side, ref in enumerate(piece):
            places_vmem[2 * e + side] = places_of(ref)
    places_copy = pltpu.make_async_copy(places_vmem, places, places_sem)
    places_copy.start()
    total[...] = jnp.zeros_like(total)
    start = 0
    for ref in b_refs:
        size = ref.shape[0]
        b_all[pl.ds(start, size)] = ref[...]
        start += size

    def order_rows(from_chip, first_core, into):
        for side in range(2):
            for k in range(col_tiles):
                place = first_core if side == 0 else 1 - first_core
                tile = order_ref[(from_chip * 2 + place) * col_tiles + k]
                at = ((tile // b_tiles) ^ row) * b_tiles + tile % b_tiles
                into[pl.ds((side * col_tiles + k) * TILE, TILE)] = b_all[
                    pl.ds(pl.multiple_of(at * TILE, TILE), TILE)
                ]

    order_rows(jnp.where(chip == 0, chips - 1, 0), 0, far_rows)
    places_copy.wait()

    for e, step in enumerate(steps):
        source = chip + (2 * core - 1) * step

        @pl.when((source >= 0) & (source < chips))
        def _(e=e, step=step, source=source):
            order_rows(source, core if step >= 0 else 1 - core, ordered)

            @pl.loop(0, total.shape[0] // ROWS)
            def _(m):
                at = pl.ds(pl.multiple_of(m * ROWS, ROWS), ROWS)
                left = [
                    unpacked(places, 2 * e + side, m, pieces[e][side], col_tiles)
                    for side in range(2)
                ]
                total[at] += dot(jnp.concatenate(left, axis=1), ordered[...])


def near(chips, row_devices, steps, order, pieces, b_parts, shape, col_tiles):
    local_rows, result_cols = shape
    dtype = b_parts[0].dtype
    depth = 2 * col_tiles * TILE
    flat = [chunk for piece in pieces for chunk in piece] + b_parts
    blocks = 2 * len(steps)
    b_rows = sum(part.shape[0] for part in b_parts)
    scratch = [
        ((b_rows, result_cols), dtype),
        ((depth, result_cols), dtype),
        ((blocks, 8, LANES), jnp.int32),
    ]
    outs = [(shape, jnp.float32), ((depth, result_cols), dtype)]
    return pl.pallas_call(
        functools.partial(near_kernel, chips, row_devices, steps, len(b_parts)),
        out_shape=[pltpu.VMEM(*entry) for entry in outs],
        in_specs=[SMEM] + [VMEM] * len(flat),
        out_specs=[VMEM] * 2,
        scratch_shapes=[pltpu.VMEM(*entry) for entry in scratch] + [
            pltpu.SMEM((blocks, 8, LANES), jnp.int32),
            pltpu.SemaphoreType.DMA,
        ],
        compiler_params=with_vmem(scratch),
        cost_estimate=pl.CostEstimate(flops=0, bytes_accessed=0, transcendentals=0),
        name="near",
    )(in_hbm(order), *[in_vmem(x) for x in flat])


def far_kernel(chips, block, last, mine, other, far_rows, total_in, total_out, *refs):
    refs = list(refs)
    total = refs.pop(0) if last else total_out
    places_vmem, places, places_sem = refs[:3]
    col = lax.axis_index("col")
    chip, core = col // 2, col % 2
    depth = far_rows.shape[0] // 2
    height = LAST_ROWS if last else ROWS
    outs = [None] * (total.shape[0] // height)
    if last:
        for m in range(len(outs)):
            at = pl.ds(m * height, height)
            outs[m] = pltpu.make_async_copy(total.at[at], total_out.at[at], refs[3].at[m])

    for ref, stream in ((mine, core), (other, 1 - core)):

        @pl.when(chip == (chips - 1) * (1 - stream))
        def _(ref=ref, stream=stream):
            places_vmem[...] = places_of(ref)
            copy = pltpu.make_async_copy(places_vmem, places.at[0], places_sem)
            copy.start()
            start = pl.multiple_of((stream ^ block) * depth, depth)
            right = far_rows[pl.ds(start, depth)]
            copy.wait()
            for m, out in enumerate(outs):
                at = pl.ds(m * height, height)
                left = unpacked(places, 0, m, ref, depth // TILE, height)
                total[at] = total_in[at] + dot(left, right)
                if last:
                    out.start()

    if last:

        @pl.when((chip != 0) & (chip != chips - 1))
        def _():
            for m, out in enumerate(outs):
                at = pl.ds(m * height, height)
                total[at] = total_in[at]
                out.start()

        for out in outs:
            out.wait()


def far(chips, block, mine, other, far_rows, total, last):
    shape = total.shape
    local_rows, result_cols = shape
    scratch = [((8, LANES), jnp.int32)]
    if last:
        scratch.insert(0, (shape, jnp.float32))
    sems = [pltpu.SemaphoreType.DMA((local_rows // LAST_ROWS,))] if last else []
    return pl.pallas_call(
        functools.partial(far_kernel, chips, block, last),
        out_shape=(pltpu.HBM if last else pltpu.VMEM)(shape, jnp.float32),
        in_specs=[VMEM] * 4,
        out_specs=ANY if last else VMEM,
        input_output_aliases={} if last else {3: 0},
        scratch_shapes=[pltpu.VMEM(*entry) for entry in scratch] + [
            pltpu.SMEM((1, 8, LANES), jnp.int32),
            pltpu.SemaphoreType.DMA,
        ] + sems,
        compiler_params=with_vmem(scratch),
        cost_estimate=pl.CostEstimate(
            flops=local_rows * result_cols * far_rows.shape[0], bytes_accessed=8 * 1024 * 1024,
            transcendentals=0,
        ),
        name="far",
    )(*[in_vmem(x) for x in (mine, other, far_rows, total)])


def after(chunk, others):
    return lax.optimization_barrier((chunk, *others))[0] if others else chunk


class Transfers:
    def __init__(self, row_devices, chips, own, integrals):
        self.row_devices = row_devices
        self.chips = chips
        self.integrals = integrals
        self.made = {("own", 0, 0): own, ("side", 0, 0): integrals}

    def get(self, name):
        if name not in self.made:
            self.made[name] = getattr(self, name[0])(name, *name[1:])
        return self.made[name]

    def held(self, name):
        return name[1] < (self.row_devices if name[0] == "side" else self.chips)

    def send(self, chunk, axis, perm, name):
        others = [self.get(other) for other in ORDER.get(name, ()) if self.held(other)]
        return lax.ppermute(after(chunk, others), axis, perm)

    def line(self, name, step, i):
        cross = i if step == 1 else 0
        below, above = range(step, self.chips), range(self.chips - step)
        perm = [(2 * (z - 1) + cross, 2 * z) for z in below]
        perm += [(2 * (z + 1) + 1 - cross, 2 * z + 1) for z in above]
        chunk = self.get(("own", 0, 0) if step == 1 else ("line", step - 1, i))
        return self.send(chunk, "col", perm, name)

    def swap(self, name, step, i):
        perm = [(2 * z, 2 * z + 1) for z in range(step, self.chips)]
        perm += [(2 * z + 1, 2 * z) for z in range(self.chips - step)]
        chunk = self.get(("line", step, i) if step else ("own", 0, 0))[:SWAP]
        return self.send(chunk, "col", perm, name)

    def half(self, d, h):
        if d & (d - 1):
            return self.get(("side", d, h))
        rows = self.integrals.shape[0] // 2
        return self.get(("side", d, 0))[h * rows : (h + 1) * rows]

    def side(self, name, d, h):
        if d & (d - 1):
            bit = d & -d if h else 1 << (d.bit_length() - 1)
            chunk = self.half(d ^ bit, h)
        else:
            bit, chunk = d, self.integrals
        perm = [(r, r ^ bit) for r in range(self.row_devices)]
        return self.send(chunk, "row", perm, name)


def local(row_devices, col_devices, amplitudes, integrals, screen_mask, tile_order):
    chips = col_devices // 2
    own = pack(screen_mask, amplitudes)
    moves = Transfers(row_devices, chips, own, integrals)
    sides = [("side", d, h) for d in range(row_devices) for h in range(2 if d & (d - 1) else 1)]
    steps = [0]
    pieces = [(own, moves.get(("swap", 0, 0)))]
    for step in range(1, chips - 1):
        for kind in ("line", "swap"):
            steps.append(step if kind == "line" else -step)
            pieces.append([moves.get((kind, step, i)) for i in range(2)])
    total, far_rows = near(
        chips, row_devices, steps, tile_order, pieces, [moves.get(side) for side in sides],
        (amplitudes.shape[0], integrals.shape[1]), screen_mask.shape[1],
    )
    last = []
    for i in range(2):
        name = ("line", chips - 1, i)
        moves.made[name], total = lax.optimization_barrier((moves.get(name), total))
        last.append((moves.made[name], moves.get(("swap", chips - 1, i))))
    for i, (block, other) in enumerate(last):
        total = far(chips, i, block, other, far_rows, total, i == len(last) - 1)
    return total


def solution(mesh):
    placed = (P("row", "col"), P("row", "col"), P("row", "col"), P())
    return jax.shard_map(
        functools.partial(local, mesh.shape["row"], mesh.shape["col"]),
        mesh=mesh, in_specs=placed, out_specs=P("row", "col"), check_vma=False,
    )
```
